32 devices in a mesh: band: 16 (over z, x, core), slab: 2 (over y).
Axes of the slice: x: 2, y: 2, z: 4, core: 2. Of those that a mesh axis runs over, the one named last changes fastest.
Arguments:
- orbitals: float32 [64, 96, 4608], P('band', 'slab'), may hold values from -3 to 3
- owner: int32 [2], replicated, may hold values from 0 to 15
- picks: int32 [2, 2], replicated, may hold values from 0 to 3
Outputs:
- exchange_field: float32 [64, 96, 4608], P('band', 'slab')
- transposed: float32 [2, 2, 96, 4608], P(None, None, 'slab')
The draws below stay inside these ranges and needn't reach their ends.
Inputs may be any that keep to these rules, and one draw needn't show every extreme that they name: owner names a band group and picks positions within it; the two picks of a step may coincide.
All inputs are finite; a program needn't handle non-finite values.
Results may differ from the reference program's by a relative error of at most 0.0001.
Values sent between devices are 32-bit elements; how exact they have to be, the bound alone decides.
A program may use at most 128 MiB of HBM per device.

```python
import math
import jax
import jax.numpy as jnp
from jax import lax

NX = 48
NY = 96
NZ = 96
BLOC = 4
STEPS = 2
BANDS = 64
N_BAND = 16


def touch_ends(array, own_key, least, largest):
    longest = array.shape.index(max(array.shape))
    spots = []
    for shift in (0, 1):
        where = [jax.random.randint(jax.random.fold_in(own_key, axis), (), 0, length) for axis, length in enumerate(array.shape)]
        where[longest] = (where[longest] + shift) % array.shape[longest]
        spots.append(tuple(where))
    return array.at[spots[0]].set(least).at[spots[1]].set(largest)


def block_levels(rng, extent, shards, low, top_value):
    gain, own = 1.0, jax.random.fold_in(rng, 6)
    for axis_at, blocks in shards:
        heights = jnp.exp(jax.random.uniform(jax.random.fold_in(own, axis_at), (blocks,), jnp.float32, low / len(shards), top_value / len(shards)))
        gain = gain * jnp.repeat(heights, extent[axis_at] // blocks).reshape([-1 if axis == axis_at else 1 for axis in range(len(extent))])
    return gain


def noise(own_key, extent, deviation, limit, shards=(), kind=jnp.bfloat16):
    array = deviation * jax.random.normal(own_key, extent, jnp.float32)
    if shards:
        array = array * block_levels(own_key, extent, shards, -0.22, 0.18)
    return jnp.clip(array, -limit, limit).astype(kind)


def setup_inputs(seed: int = 0) -> dict:
    seeds = jax.random.split(jax.random.key(seed), 4)
    orbitals = noise(seeds[0], (BANDS, NZ, NY * NX), 0.5, 3.0, ((0, 16), (1, 2)), jnp.float32)
    owner = jax.random.randint(seeds[1], (STEPS,), 0, N_BAND).astype(jnp.int32)
    picks = touch_ends(jax.random.randint(seeds[2], (STEPS, 2), 0, BLOC), jax.random.fold_in(seeds[2], 1), 0, BLOC - 1).astype(jnp.int32)
    return dict(orbitals=orbitals, owner=owner, picks=picks)


length_first = 41.05
length_side = 41.05
length_last = 20.525
omega_screen = 0.106


def frequency(counter, length):
    return jnp.where(counter <= length // 2, counter, counter - length).astype(jnp.float32)


def coulomb_kernel(freq_z, freq_y, freq_x):
    wave_first = 2.0 * math.pi / length_first
    wave_side = 2.0 * math.pi / length_side
    wave_last = 2.0 * math.pi / length_last
    squared = (wave_first * freq_z)[:, None, None] ** 2 + (wave_side * freq_y)[None, :, None] ** 2 + (wave_last * freq_x)[None, None, :] ** 2
    safe = jnp.where(squared > 0, squared, 1.0)
    screened = -4.0 * math.pi * jnp.expm1(-squared / (4.0 * omega_screen ** 2)) / safe
    return jnp.where(squared > 0, screened, math.pi / omega_screen ** 2)


def reference(orbitals, owner, picks):
    kernel = coulomb_kernel(frequency(jnp.arange(NZ), NZ), frequency(jnp.arange(NY), NY), frequency(jnp.arange(NX), NX))
    exchange_sum = jnp.zeros_like(orbitals)
    collected = []
    for turn_index in range(STEPS):
        chosen_rows = (owner[turn_index] * BLOC + picks[turn_index]).astype(jnp.int32)
        chosen = jnp.take(orbitals, chosen_rows, axis=0)

        def accumulate(running, orbital):
            density = lax.complex(orbital * chosen[0], orbital * chosen[1]).reshape(NZ, NY, NX)
            potential = jnp.fft.ifftn(kernel * jnp.fft.fftn(density)).reshape(NZ, NY * NX)
            first_part = jnp.real(potential)
            second_part = jnp.imag(potential)
            running = running + jnp.stack([first_part * orbital, second_part * orbital])
            return running, first_part * chosen[0] + second_part * chosen[1]

        start_sum = jnp.zeros((2, NZ, NY * NX), orbitals.dtype)
        summed, applied = lax.scan(accumulate, start_sum, orbitals)
        exchange_sum = exchange_sum + applied
        collected.append(summed)
    return exchange_sum, jnp.stack(collected)
```

```python
import functools
import math

import jax
import jax.numpy as jnp
import numpy as np
from jax import lax
from jax.experimental import pallas as pl
from jax.experimental.pallas import tpu as pltpu
from jax.sharding import PartitionSpec as P

NX = 48
NY = 96
NZ = 96
STEPS = 2
OUTER = 12
INNER = 8
WIDE = INNER * NX
SIN60 = math.sqrt(3.0) / 2.0


length_first = 41.05
length_side = 41.05
length_last = 20.525
omega_screen = 0.106


def split_table(table):
    high = table.astype(jnp.bfloat16)
    low = (table - high.astype(np.float64)).astype(jnp.bfloat16)
    return high, low


def unit_table(rows, columns, length):
    angle = 2.0 * np.pi / length * (np.outer(rows, columns) % length)
    return np.cos(angle), np.sin(angle)


def plane_table():
    cy, sy = unit_table(np.arange(INNER), np.arange(INNER), INNER)
    cx, sx = unit_table(np.arange(NX), np.arange(NX), NX)
    cosines = np.kron(cy, cx) - np.kron(sy, sx)
    sines = np.kron(cy, sx) + np.kron(sy, cx)
    high, low = split_table(np.block([[cosines, -sines], [sines, cosines]]))
    return np.concatenate([high, high, low], axis=0)


def first_table(direction):
    cosines, sines = unit_table(np.arange(NZ), np.arange(NZ), NZ)
    sines = direction * sines
    high, low = split_table(np.block([[cosines, sines], [-sines, cosines]]))
    return np.concatenate([high, low, high], axis=1)


def twiddle_table():
    cosines, sines = unit_table(np.arange(OUTER), np.repeat(np.arange(INNER), NX), NY)
    return np.stack([cosines, sines]).astype(np.float32)


def screened_table():
    def signed(length):
        counter = np.arange(length)
        return np.where(counter <= length // 2, counter, counter - length).astype(np.float64)

    gz = 2.0 * math.pi / length_first * signed(NZ)
    gy = 2.0 * math.pi / length_side * signed(NY)
    gx = 2.0 * math.pi / length_last * signed(NX)
    squared = gz[:, None, None] ** 2 + gy[None, :, None] ** 2 + gx[None, None, :] ** 2
    safe = np.where(squared > 0, squared, 1.0)
    screened = -4.0 * math.pi * np.expm1(-squared / (4.0 * omega_screen**2)) / safe
    kernel = np.where(squared > 0, screened, math.pi / omega_screen**2) / (NX * NY * NZ)
    kernel = kernel.reshape(NZ, INNER, OUTER, NX).transpose(2, 0, 1, 3)
    return kernel.reshape(OUTER * NZ, WIDE).astype(np.float32)


def transform3(parts):
    (r0, i0), (r1, i1), (r2, i2) = parts
    sr, si = r1 + r2, i1 + i2
    dr, di = SIN60 * (r1 - r2), SIN60 * (i1 - i2)
    mr, mi = r0 - 0.5 * sr, i0 - 0.5 * si
    return [(r0 + sr, i0 + si), (mr + di, mi - dr), (mr - di, mi + dr)]


def transform4(parts):
    (r0, i0), (r1, i1), (r2, i2), (r3, i3) = parts
    ar, ai, br, bi = r0 + r2, i0 + i2, r0 - r2, i0 - i2
    cr, ci, dr, di = r1 + r3, i1 + i3, r1 - r3, i1 - i3
    return [(ar + cr, ai + ci), (br + di, bi - dr), (ar - cr, ai - ci), (br - di, bi + dr)]


def transform12(values):
    rows = []
    for n2 in range(4):
        rows.append(transform3([values[(4 * n1 + 3 * n2) % 12] for n1 in range(3)]))
    out = [None] * 12
    for k1 in range(3):
        column = transform4([rows[n2][k1] for n2 in range(4)])
        for k2 in range(4):
            out[(4 * k1 + 9 * k2) % 12] = column[k2]
    return out


def swapped(values):
    return [(im, re) for re, im in values]


def halves(value):
    high = value.astype(jnp.bfloat16)
    return high, (value - high.astype(jnp.float32)).astype(jnp.bfloat16)


def put(split_ref, rows, column, value):
    high, low = halves(value)
    width = value.shape[-1]
    split_ref[rows, pl.ds(column, width)] = high
    split_ref[rows, pl.ds(2 * WIDE + column, width)] = low
    split_ref[rows, pl.ds(4 * WIDE + column, width)] = high


def potential_kernel(has_previous, *refs):
    refs = list(refs)
    plane_ref, forth_ref, back_ref, twiddle_ref, screen_ref = refs[:5]
    orbital_refs, chosen_refs = refs[5:7], refs[7:9]
    at = 9
    previous_refs = [None, None]
    if has_previous:
        previous_refs = refs[at : at + 2]
        at += 2
    applied_refs, summed_refs = refs[at : at + 2], refs[at + 2 : at + 4]
    split_ref, field_ref = refs[at + 4 : at + 6]
    planes = orbital_refs[0].shape[1]
    tall = 16

    for part in range(2):
        for lane in range(0, WIDE, 128):

            @pl.loop(0, planes // tall)
            def _(step, part=part, lane=lane):
                start = pl.multiple_of(step * tall, tall)
                here = pl.ds(start, tall)
                values = []
                for outer in range(OUTER):
                    cols = pl.ds(outer * WIDE + lane, 128)
                    orbital = orbital_refs[part][0, here, cols]
                    values.append((orbital * chosen_refs[part][0, here, cols], orbital * chosen_refs[part][1, here, cols]))
                for k1, (re, im) in enumerate(transform12(values)):
                    if k1:
                        tc = twiddle_ref[0, pl.ds(k1, 1), pl.ds(lane, 128)]
                        ts = twiddle_ref[1, pl.ds(k1, 1), pl.ds(lane, 128)]
                        re, im = re * tc + im * ts, im * tc - re * ts
                    rows = pl.ds(pl.multiple_of(k1 * NZ + part * planes + start, tall), tall)
                    put(split_ref, rows, lane, re)
                    put(split_ref, rows, WIDE + lane, im)

    def plane_pass():
        chunk = 384

        @pl.loop(0, OUTER * NZ // chunk)
        def _(step):
            rows = pl.ds(pl.multiple_of(step * chunk, chunk), chunk)
            field_ref[rows, :] = jnp.dot(split_ref[rows, :], plane_ref[...], preferred_element_type=jnp.float32)

    plane_pass()

    @pl.loop(0, OUTER)
    def _(k1):
        rows = pl.ds(pl.multiple_of(k1 * NZ, NZ), NZ)
        field = jnp.concatenate([field_ref[rows, :WIDE], field_ref[rows, WIDE:]], axis=0)
        high, low = halves(field)
        field = jnp.dot(forth_ref[...], jnp.concatenate([high, high, low], axis=0), preferred_element_type=jnp.float32)
        screen = screen_ref[rows, :]
        field = field * jnp.concatenate([screen, screen], axis=0)
        high, low = halves(field)
        field = jnp.dot(back_ref[...], jnp.concatenate([high, high, low], axis=0), preferred_element_type=jnp.float32)
        put(split_ref, rows, 0, field[NZ:])
        put(split_ref, rows, WIDE, field[:NZ])

    plane_pass()

    @pl.when(pl.program_id(0) == 0)
    def _():
        for summed_ref in summed_refs:
            summed_ref[...] = jnp.zeros_like(summed_ref)

    for part in range(2):
        for lane in range(0, WIDE, 128):

            @pl.loop(0, planes // 8)
            def _(step, part=part, lane=lane):
                start = pl.multiple_of(step * 8, 8)
                here = pl.ds(start, 8)
                values = []
                for k1 in range(OUTER):
                    rows = pl.ds(pl.multiple_of(k1 * NZ + part * planes + start, 8), 8)
                    im = field_ref[rows, pl.ds(lane, 128)]
                    re = field_ref[rows, pl.ds(WIDE + lane, 128)]
                    if k1:
                        tc = twiddle_ref[0, pl.ds(k1, 1), pl.ds(lane, 128)]
                        ts = twiddle_ref[1, pl.ds(k1, 1), pl.ds(lane, 128)]
                        re, im = re * tc - im * ts, re * ts + im * tc
                    values.append((re, im))
                for outer, (first, second) in enumerate(swapped(transform12(swapped(values)))):
                    cols = pl.ds(outer * WIDE + lane, 128)
                    orbital = orbital_refs[part][0, here, cols]
                    applied = first * chosen_refs[part][0, here, cols] + second * chosen_refs[part][1, here, cols]
                    if has_previous:
                        applied = applied + previous_refs[part][0, here, cols]
                    applied_refs[part][0, here, cols] = applied
                    summed_refs[part][0, here, cols] += first * orbital
                    summed_refs[part][1, here, cols] += second * orbital


def potentials(orbital_parts, chosen_parts, previous_parts):
    count, planes, points = orbital_parts[0].shape
    tables = [plane_table(), first_table(1.0), first_table(-1.0), twiddle_table(), screened_table()]
    tables = [jnp.asarray(table) for table in tables]
    has_previous = previous_parts is not None

    def whole(shape):
        return pl.BlockSpec(shape, lambda band: (0,) * len(shape))

    per_band = pl.BlockSpec((1, planes, points), lambda band: (band, 0, 0))
    pair = whole((2, planes, points))
    inputs = tables + list(orbital_parts) + list(chosen_parts) + (list(previous_parts) if has_previous else [])
    in_specs = [whole(table.shape) for table in tables] + [per_band] * 2 + [pair] * 2 + [per_band] * (2 * has_previous)
    band_shape = jax.ShapeDtypeStruct((count, planes, points), jnp.float32)
    pair_shape = jax.ShapeDtypeStruct((2, planes, points), jnp.float32)
    rows = OUTER * NZ
    flops = count * (2 * 2 * rows * 6 * WIDE * 2 * WIDE + 2 * 2 * 2 * NZ * 6 * NZ * OUTER * WIDE)
    moved = 4 * planes * points * (2 * count * (2 + has_previous) + 8 + 2)
    return pl.pallas_call(
        functools.partial(potential_kernel, has_previous),
        grid=(count,),
        out_shape=[band_shape] * 2 + [pair_shape] * 2,
        in_specs=in_specs,
        out_specs=[per_band] * 2 + [pair] * 2,
        scratch_shapes=[
            pltpu.VMEM((rows, 6 * WIDE), jnp.bfloat16),
            pltpu.VMEM((rows, 2 * WIDE), jnp.float32),
        ],
        compiler_params=pltpu.CompilerParams(vmem_limit_bytes=56 * 1024 * 1024, dimension_semantics=("arbitrary",)),
        cost_estimate=pl.CostEstimate(flops=2 * flops, bytes_accessed=moved, transcendentals=0),
    )(*inputs)


def whole_bands(orbitals, owner, picks):
    bloc, planes, points = orbitals.shape
    half = bloc // 2
    slab = lax.axis_index("slab")
    band = lax.axis_index("band")
    core = lax.rem(band, 2)
    groups = lax.axis_size("band")
    across = [(0, 1), (1, 0)]
    cores = [(index, index ^ 1) for index in range(groups)]

    chosen = []
    for step in range(STEPS):
        fetched = jnp.take(orbitals, picks[step], axis=0)
        fetched = jnp.where(band == owner[step], fetched, jnp.zeros_like(fetched))
        if chosen:
            fetched, chosen[-1] = lax.optimization_barrier((fetched, chosen[-1]))
        chosen.append(lax.psum(fetched, "band"))

    own = lax.dynamic_slice_in_dim(orbitals, slab * half, half, 0)
    sent = lax.dynamic_slice_in_dim(orbitals, (1 - slab) * half, half, 0)
    orbital_parts = (own, lax.ppermute(sent, "slab", across))

    applied = None
    collected = []
    for step in range(STEPS):
        row = lax.dynamic_index_in_dim(chosen[step], core, 0, keepdims=False)
        row = lax.ppermute(row, "slab", across)
        twin = lax.ppermute(row, "band", cores)
        other = jnp.where(core == 0, jnp.stack([row, twin]), jnp.stack([twin, row]))
        applied_own, applied_other, summed_own, summed_other = potentials(orbital_parts, (chosen[step], other), applied)
        applied = (applied_own, applied_other)
        keep = lax.dynamic_index_in_dim(summed_other, core, 0, keepdims=False)
        give = lax.dynamic_index_in_dim(summed_other, 1 - core, 0, keepdims=False)
        row = lax.ppermute(keep + lax.ppermute(give, "band", cores), "slab", across)
        placed = jnp.where((jnp.arange(2) == core)[:, None, None], row[None], jnp.zeros_like(row)[None])
        total = summed_own + placed
        if collected:
            total, collected[-1] = lax.optimization_barrier((total, collected[-1]))
        collected.append(lax.psum(total, "band"))
    back = lax.ppermute(applied[1], "slab", across)
    exchange = jnp.where(slab == 0, jnp.concatenate([applied[0], back]), jnp.concatenate([back, applied[0]]))
    return exchange, jnp.stack(collected)


def broadcast(x, axis, root):
    mine = lax.axis_index(axis) == root
    return lax.psum(jnp.where(mine, x, jnp.zeros_like(x)), axis)


def frequency(counter, length):
    return jnp.where(counter <= length // 2, counter, counter - length).astype(jnp.float32)


def coulomb_kernel(freq_z, freq_y, freq_x):
    wave_first = 2.0 * math.pi / length_first
    wave_side = 2.0 * math.pi / length_side
    wave_last = 2.0 * math.pi / length_last
    squared = (
        (wave_first * freq_z)[:, None, None] ** 2
        + (wave_side * freq_y)[None, :, None] ** 2
        + (wave_last * freq_x)[None, None, :] ** 2
    )
    safe = jnp.where(squared > 0, squared, 1.0)
    screened = -4.0 * math.pi * jnp.expm1(-squared / (4.0 * omega_screen**2)) / safe
    return jnp.where(squared > 0, screened, math.pi / omega_screen**2)


def dft_table(length, direction):
    counter = jnp.arange(length)
    product = counter[:, None] * counter[None, :] % length
    angle = 2.0 * math.pi / length * product.astype(jnp.float32)
    return (jnp.cos(angle), direction * jnp.sin(angle))


def along_last(values, length, direction):
    cosines, sine_table = dft_table(length, direction)
    upper = jnp.concatenate([cosines, -sine_table], axis=1)
    lower = jnp.concatenate([sine_table, cosines], axis=1)
    matrix = jnp.concatenate([upper, lower], axis=0)
    return jnp.matmul(values, matrix, precision=lax.Precision.HIGHEST)


def along_axis(values, length, direction, pattern):
    cosines, sine_table = dft_table(length, direction)
    middle = values.shape[-1] // 2
    with_cos = jnp.einsum(pattern, cosines, values, precision=lax.Precision.HIGHEST)
    with_sin = jnp.einsum(pattern, sine_table, values, precision=lax.Precision.HIGHEST)
    real_part = with_cos[..., :middle] + with_sin[..., middle:]
    imag_part = with_cos[..., middle:] - with_sin[..., :middle]
    return jnp.concatenate([real_part, imag_part], axis=-1)


def per_device(orbitals, owner, picks):
    bloc, planes, points = orbitals.shape
    slab_count = lax.axis_size("slab")
    column_rows = NY // slab_count
    slab_index = lax.axis_index("slab")
    freq_y = frequency(slab_index * column_rows + jnp.arange(column_rows), NY)
    kernel = coulomb_kernel(frequency(jnp.arange(NZ), NZ), freq_y, frequency(jnp.arange(NX), NX))
    kernel = kernel * (1.0 / (NX * NY * NZ))
    kernel_tile = jnp.concatenate([kernel, kernel], axis=-1)
    exchange_sum = jnp.zeros_like(orbitals)
    collected = []
    for turn_index in range(STEPS):
        fetch_chosen = jnp.take(orbitals, picks[turn_index], axis=0)
        chosen = broadcast(fetch_chosen, "band", owner[turn_index])
        real_part = (orbitals * chosen[0]).reshape(bloc, planes, NY, NX)
        imag_part = (orbitals * chosen[1]).reshape(bloc, planes, NY, NX)
        fields = jnp.concatenate([real_part, imag_part], axis=-1)
        fields = along_last(fields, NX, 1.0)
        fields = along_axis(fields, NY, 1.0, "ky,bzyx->bzkx")
        columns = lax.all_to_all(fields, "slab", split_axis=2, concat_axis=1, tiled=True)
        columns = along_axis(columns, NZ, 1.0, "kz,bzyx->bkyx") * kernel_tile
        columns = along_axis(columns, NZ, -1.0, "kz,bzyx->bkyx")
        fields = lax.all_to_all(columns, "slab", split_axis=1, concat_axis=2, tiled=True)
        fields = along_axis(fields, NY, -1.0, "ky,bzyx->bzkx")
        fields = along_last(fields, NX, -1.0)
        count = fields.shape[0]
        potentials_first_part = fields[..., :NX].reshape(count, planes, points)
        potentials_second_part = fields[..., NX:].reshape(count, planes, points)
        applied = potentials_first_part * chosen[0] + potentials_second_part * chosen[1]
        contributions_local_sum = jnp.stack(
            [
                jnp.sum(potentials_first_part * orbitals, axis=0),
                jnp.sum(potentials_second_part * orbitals, axis=0),
            ]
        )
        applied, local_sum = (applied, contributions_local_sum)
        exchange_sum = exchange_sum + applied
        collected.append(lax.psum(local_sum, "band"))
    transposed = jnp.stack(collected)
    return (exchange_sum, transposed)


def solution(mesh):
    body = whole_bands if mesh.shape["slab"] == 2 and mesh.shape["band"] % 2 == 0 else per_device
    in_specs = (P("band", "slab", None), P(), P())
    out_specs = (P("band", "slab", None), P(None, None, "slab", None))
    return jax.shard_map(body, mesh=mesh, in_specs=in_specs, out_specs=out_specs, check_vma=False)
```

```python
import functools
import math

import jax
import jax.numpy as jnp
import numpy as np
from jax import lax
from jax.experimental import pallas as pl
from jax.experimental.pallas import tpu as pltpu
from jax.sharding import PartitionSpec as P

NX = 48
NY = 96
NZ = 96
STEPS = 2
OUTER = 12
INNER = 8
WIDE = INNER * NX
SIN60 = math.sqrt(3.0) / 2.0


length_first = 41.05
length_side = 41.05
length_last = 20.525
omega_screen = 0.106


def split_table(table):
    high = table.astype(jnp.bfloat16)
    low = (table - high.astype(np.float64)).astype(jnp.bfloat16)
    return high, low


def unit_table(rows, columns, length):
    angle = 2.0 * np.pi / length * (np.outer(rows, columns) % length)
    return np.cos(angle), np.sin(angle)


def plane_table():
    cy, sy = unit_table(np.arange(INNER), np.arange(INNER), INNER)
    cx, sx = unit_table(np.arange(NX), np.arange(NX), NX)
    cosines = np.kron(cy, cx) - np.kron(sy, sx)
    sines = np.kron(cy, sx) + np.kron(sy, cx)
    high, low = split_table(np.block([[cosines, -sines], [sines, cosines]]))
    return np.concatenate([high, high, low], axis=0)


def first_table(direction):
    cosines, sines = unit_table(np.arange(NZ), np.arange(NZ), NZ)
    sines = direction * sines
    high, low = split_table(np.block([[cosines, sines], [-sines, cosines]]))
    return np.concatenate([high, low, high], axis=1)


def twiddle_table():
    cosines, sines = unit_table(np.arange(OUTER), np.repeat(np.arange(INNER), NX), NY)
    return np.stack([cosines, sines]).astype(np.float32)


def screened_table():
    def signed(length):
        counter = np.arange(length)
        return np.where(counter <= length // 2, counter, counter - length).astype(np.float64)

    gz = 2.0 * math.pi / length_first * signed(NZ)
    gy = 2.0 * math.pi / length_side * signed(NY)
    gx = 2.0 * math.pi / length_last * signed(NX)
    squared = gz[:, None, None] ** 2 + gy[None, :, None] ** 2 + gx[None, None, :] ** 2
    safe = np.where(squared > 0, squared, 1.0)
    screened = -4.0 * math.pi * np.expm1(-squared / (4.0 * omega_screen**2)) / safe
    kernel = np.where(squared > 0, screened, math.pi / omega_screen**2) / (NX * NY * NZ)
    kernel = kernel.reshape(NZ, INNER, OUTER, NX).transpose(2, 0, 1, 3)
    return kernel.reshape(OUTER * NZ, WIDE).astype(np.float32)


def transform3(parts):
    (r0, i0), (r1, i1), (r2, i2) = parts
    sr, si = r1 + r2, i1 + i2
    dr, di = SIN60 * (r1 - r2), SIN60 * (i1 - i2)
    mr, mi = r0 - 0.5 * sr, i0 - 0.5 * si
    return [(r0 + sr, i0 + si), (mr + di, mi - dr), (mr - di, mi + dr)]


def transform4(parts):
    (r0, i0), (r1, i1), (r2, i2), (r3, i3) = parts
    ar, ai, br, bi = r0 + r2, i0 + i2, r0 - r2, i0 - i2
    cr, ci, dr, di = r1 + r3, i1 + i3, r1 - r3, i1 - i3
    return [(ar + cr, ai + ci), (br + di, bi - dr), (ar - cr, ai - ci), (br - di, bi + dr)]


def transform12(values):
    rows = []
    for n2 in range(4):
        rows.append(transform3([values[(4 * n1 + 3 * n2) % 12] for n1 in range(3)]))
    out = [None] * 12
    for k1 in range(3):
        column = transform4([rows[n2][k1] for n2 in range(4)])
        for k2 in range(4):
            out[(4 * k1 + 9 * k2) % 12] = column[k2]
    return out


def swapped(values):
    return [(im, re) for re, im in values]


def halves(value):
    high = value.astype(jnp.bfloat16)
    return high, (value - high.astype(jnp.float32)).astype(jnp.bfloat16)


def put(split_ref, rows, column, value):
    high, low = halves(value)
    width = value.shape[-1]
    split_ref[rows, pl.ds(column, width)] = high
    split_ref[rows, pl.ds(2 * WIDE + column, width)] = low
    split_ref[rows, pl.ds(4 * WIDE + column, width)] = high


def potential_kernel(*refs):
    plane_ref, forth_ref, back_ref, twiddle_ref, screen_ref = refs[:5]
    orbital_refs, chosen_refs = refs[5:7], refs[7:9]
    applied_refs, summed_refs = refs[9:11], refs[11:13]
    split_ref, field_ref = refs[13:15]
    turn = pl.program_id(1)
    planes = orbital_refs[0].shape[1]
    tall = 16

    for part in range(2):
        for lane in range(0, WIDE, 128):

            @pl.loop(0, planes // tall)
            def _(step, part=part, lane=lane):
                start = pl.multiple_of(step * tall, tall)
                here = pl.ds(start, tall)
                values = []
                for outer in range(OUTER):
                    cols = pl.ds(outer * WIDE + lane, 128)
                    orbital = orbital_refs[part][0, here, cols]
                    values.append((orbital * chosen_refs[part][0, 0, 0, here, cols], orbital * chosen_refs[part][0, 0, 1, here, cols]))
                for k1, (re, im) in enumerate(transform12(values)):
                    if k1:
                        tc = twiddle_ref[0, pl.ds(k1, 1), pl.ds(lane, 128)]
                        ts = twiddle_ref[1, pl.ds(k1, 1), pl.ds(lane, 128)]
                        re, im = re * tc + im * ts, im * tc - re * ts
                    rows = pl.ds(pl.multiple_of(k1 * NZ + part * planes + start, tall), tall)
                    put(split_ref, rows, lane, re)
                    put(split_ref, rows, WIDE + lane, im)

    def plane_pass():
        chunk = 384

        @pl.loop(0, OUTER * NZ // chunk)
        def _(step):
            rows = pl.ds(pl.multiple_of(step * chunk, chunk), chunk)
            field_ref[rows, :] = jnp.dot(split_ref[rows, :], plane_ref[...], preferred_element_type=jnp.float32)

    plane_pass()

    @pl.loop(0, OUTER)
    def _(k1):
        rows = pl.ds(pl.multiple_of(k1 * NZ, NZ), NZ)
        field = jnp.concatenate([field_ref[rows, :WIDE], field_ref[rows, WIDE:]], axis=0)
        high, low = halves(field)
        field = jnp.dot(forth_ref[...], jnp.concatenate([high, high, low], axis=0), preferred_element_type=jnp.float32)
        screen = screen_ref[rows, :]
        field = field * jnp.concatenate([screen, screen], axis=0)
        high, low = halves(field)
        field = jnp.dot(back_ref[...], jnp.concatenate([high, high, low], axis=0), preferred_element_type=jnp.float32)
        put(split_ref, rows, 0, field[NZ:])
        put(split_ref, rows, WIDE, field[:NZ])

    plane_pass()

    @pl.when(pl.program_id(0) == 0)
    def _():
        for summed_ref in summed_refs:
            summed_ref[turn] = jnp.zeros(summed_ref.shape[1:], jnp.float32)

    for part in range(2):
        for lane in range(0, WIDE, 128):

            @pl.loop(0, planes // 8)
            def _(step, part=part, lane=lane):
                start = pl.multiple_of(step * 8, 8)
                here = pl.ds(start, 8)
                values = []
                for k1 in range(OUTER):
                    rows = pl.ds(pl.multiple_of(k1 * NZ + part * planes + start, 8), 8)
                    im = field_ref[rows, pl.ds(lane, 128)]
                    re = field_ref[rows, pl.ds(WIDE + lane, 128)]
                    if k1:
                        tc = twiddle_ref[0, pl.ds(k1, 1), pl.ds(lane, 128)]
                        ts = twiddle_ref[1, pl.ds(k1, 1), pl.ds(lane, 128)]
                        re, im = re * tc - im * ts, re * ts + im * tc
                    values.append((re, im))
                for outer, (first, second) in enumerate(swapped(transform12(swapped(values)))):
                    cols = pl.ds(outer * WIDE + lane, 128)
                    orbital = orbital_refs[part][0, here, cols]
                    applied = first * chosen_refs[part][0, 0, 0, here, cols] + second * chosen_refs[part][0, 0, 1, here, cols]
                    before = applied_refs[part][0, here, cols]
                    applied_refs[part][0, here, cols] = jnp.where(turn == 0, applied, applied + before)
                    summed_refs[part][turn, 0, here, cols] += first * orbital
                    summed_refs[part][turn, 1, here, cols] += second * orbital


def potentials(orbital_parts, chosen):
    count, planes, points = orbital_parts[0].shape
    tables = [plane_table(), first_table(1.0), first_table(-1.0), twiddle_table(), screened_table()]
    tables = [jnp.asarray(table) for table in tables]

    def constant(shape, **mode):
        return pl.BlockSpec(shape, lambda band, turn: (0,) * len(shape), **mode)

    def chosen_part(part):
        return pl.BlockSpec((1, 1, 2, planes, points), lambda band, turn: (part, turn, 0, 0, 0))

    per_band = pl.BlockSpec((1, planes, points), lambda band, turn: (band, 0, 0))
    summed = (STEPS, 2, planes, points)
    band_shape = jax.ShapeDtypeStruct((count, planes, points), jnp.float32)
    rows = OUTER * NZ
    flops = STEPS * count * (2 * 2 * rows * 6 * WIDE * 2 * WIDE + 2 * 2 * 2 * NZ * 6 * NZ * OUTER * WIDE)
    return pl.pallas_call(
        potential_kernel,
        grid=(count, STEPS),
        out_shape=[band_shape] * 2 + [jax.ShapeDtypeStruct(summed, jnp.float32)] * 2,
        in_specs=[constant(table.shape, pipeline_mode=pl.Buffered(1)) for table in tables]
        + [per_band] * 2
        + [chosen_part(0), chosen_part(1)],
        out_specs=[per_band] * 2 + [constant(summed)] * 2,
        scratch_shapes=[
            pltpu.VMEM((rows, 6 * WIDE), jnp.bfloat16),
            pltpu.VMEM((rows, 2 * WIDE), jnp.float32),
        ],
        compiler_params=pltpu.CompilerParams(
            vmem_limit_bytes=56 * 1024 * 1024, dimension_semantics=("arbitrary", "arbitrary")
        ),
        cost_estimate=pl.CostEstimate(flops=flops, bytes_accessed=4 * planes * points * 32, transcendentals=0),
    )(*tables, *orbital_parts, chosen, chosen)


RING = 8
BLOCKS = 4


def ring_band(position, core):
    x = position // 4
    z = x * (7 - 2 * position) + position
    return (z * 2 + x) * 2 + core


def ring_kernel(slabs_in, slabs_out, *refs):
    inputs = refs[: slabs_in * STEPS]
    parcel_ref, out_ref, got_ref = refs[slabs_in * STEPS : slabs_in * STEPS + 3]
    twin_ref, total_ref, ring_ref, cross_ref = refs[slabs_in * STEPS + 3 : slabs_in * STEPS + 7]
    twin_send, twin_recv, ring_send, ring_recv, lone_send, lone_recv, gather_send, gather_recv, hand_send, hand_recv = refs[
        slabs_in * STEPS + 7 :
    ]
    planes, points = inputs[0].shape[-2:]
    half, width = planes // 2, points // BLOCKS
    band, slab = lax.axis_index("band"), lax.axis_index("slab")
    core, x, z = band % 2, (band // 2) % 2, band // 4
    place = x * (7 - 2 * z) + z
    twin = {"band": band + 1 - 2 * core}
    across = {"slab": 1 - slab}
    ends = [{"band": ring_band((place + 1) % RING, core)}, {"band": ring_band((place + RING - 1) % RING, core)}]

    barrier = pltpu.get_barrier_semaphore()
    for device in [twin, across] + ends:
        pl.semaphore_signal(barrier, inc=1, device_id=device, device_id_type=pl.DeviceIdType.MESH)
    pl.semaphore_wait(barrier, 4)

    def push(source, target, send, recv, device):
        copy = pltpu.make_async_remote_copy(
            src_ref=source,
            dst_ref=target,
            send_sem=send,
            recv_sem=recv,
            device_id=device,
            device_id_type=pl.DeviceIdType.MESH,
        )
        copy.start()
        return copy

    def spot(chunk, way):
        lanes = pl.ds(pl.multiple_of((chunk % BLOCKS) * width, 128), width)
        return chunk // BLOCKS, pl.ds(way * half, half), lanes

    parcel = push(parcel_ref, got_ref, lone_send.at[0], lone_recv.at[0], across)

    swaps = []
    for at, ref in enumerate(inputs):
        swaps.append(push(ref.at[1 - core], twin_ref.at[at], twin_send.at[at], twin_recv.at[at], twin))
    for at, ref in enumerate(inputs):
        swaps[at].wait_recv()
        total_ref[at // STEPS, at % STEPS] = ref[core] + twin_ref[at]

    hops = []
    for hop in range(RING - 1):
        for way in range(2):
            sign = 1 - 2 * way
            chunk = (place + sign * (-1 - hop) + 2 * RING) % RING
            step, rows, lanes = spot(chunk, way)
            source = total_ref.at[:, step, rows, lanes]
            if hop:
                hops[-2].wait_recv()
                arrived = ring_ref.at[way, hop - 1]
                arrived[...] += total_ref[:, step, rows, lanes]
                source = arrived
            hops.append(push(source, ring_ref.at[way, hop], ring_send.at[way, hop], ring_recv.at[way, hop], ends[way]))
    step, _, lanes = spot(place, 0)
    for way in range(2):
        hops[-2 + way].wait_recv()
        _, rows, _ = spot(place, way)
        done = ring_ref[way, RING - 2] + total_ref[:, step, rows, lanes]
        out_ref[0, step, core, rows, lanes] = done[0]
        if slabs_in == 2:
            cross_ref[0, rows, :] = done[1]
    if slabs_in == 2:
        crossing = push(cross_ref.at[0], cross_ref.at[1], lone_send.at[1], lone_recv.at[1], across)
        crossing.wait_recv()
        out_ref[0, step, core, :, lanes] += cross_ref[1]
    else:
        own = out_ref.at[0, step, core, :, lanes]
        crossing = push(own, out_ref.at[1, step, core, :, lanes], lone_send.at[1], lone_recv.at[1], across)

    hands = []
    last = {}
    for hop in range(RING):
        for part in range(slabs_out):
            if hop == 0 and part == 1:
                crossing.wait_recv()
            for way in range(2):
                sign = 1 - 2 * way
                step, rows, lanes = spot((place - sign * hop + RING) % RING, way)
                if hop:
                    last[part, way].wait_recv()
                here = out_ref.at[part, step, core, rows, lanes]
                if hop < RING - 1:
                    copy = push(here, here, gather_send.at[part, way, hop], gather_recv.at[part, way, hop], ends[way])
                    last[part, way] = copy
                    hops.append(copy)
                hands.append(push(here, here, hand_send.at[part, way, hop], hand_recv.at[part, way, hop], twin))
    for copy in swaps + hops:
        copy.wait_send()
    crossing.wait_send()
    for copy in hands:
        copy.wait()
    parcel.wait()


def ring_sum(inputs, parcel, slabs_in, slabs_out, collective):
    planes, points = inputs[0].shape[-2:]
    half, width = planes // 2, points // BLOCKS
    dma = pltpu.SemaphoreType.DMA
    vmem = pl.BlockSpec(memory_space=pltpu.VMEM)
    anywhere = pl.BlockSpec(memory_space=pl.ANY)
    out = jax.ShapeDtypeStruct((slabs_out, STEPS, 2, planes, points), jnp.float32)
    return pl.pallas_call(
        functools.partial(ring_kernel, slabs_in, slabs_out),
        out_shape=[out, jax.ShapeDtypeStruct(parcel.shape, jnp.float32)],
        in_specs=[vmem] * len(inputs) + [anywhere],
        out_specs=[vmem, anywhere],
        scratch_shapes=[
            pltpu.VMEM((len(inputs), planes, points), jnp.float32),
            pltpu.VMEM((slabs_in, STEPS, planes, points), jnp.float32),
            pltpu.VMEM((2, RING - 1, slabs_in, half, width), jnp.float32),
            pltpu.VMEM((2, planes, width), jnp.float32),
            dma((len(inputs),)),
            dma((len(inputs),)),
            dma((2, RING - 1)),
            dma((2, RING - 1)),
            dma((2,)),
            dma((2,)),
            dma((slabs_out, 2, RING - 1)),
            dma((slabs_out, 2, RING - 1)),
            dma((slabs_out, 2, RING)),
            dma((slabs_out, 2, RING)),
        ],
        compiler_params=pltpu.CompilerParams(
            collective_id=collective, has_side_effects=True, vmem_limit_bytes=48 * 1024 * 1024
        ),
        cost_estimate=pl.CostEstimate(flops=0, bytes_accessed=20 * planes * points * 4, transcendentals=0),
    )(*inputs, parcel)


def whole_bands(orbitals, owner, picks):
    bloc, planes, points = orbitals.shape
    half = bloc // 2
    slab = lax.axis_index("slab")
    band = lax.axis_index("band")
    fetched = []
    for step in range(STEPS):
        rows = jnp.stack([lax.dynamic_index_in_dim(orbitals, picks[step, row], 0, keepdims=False) for row in range(2)])
        fetched.append(jnp.where(band == owner[step], rows, jnp.zeros_like(rows)))
    own = lax.dynamic_slice_in_dim(orbitals, slab * half, half, 0)
    sent = lax.dynamic_slice_in_dim(orbitals, (1 - slab) * half, half, 0)
    chosen, other = ring_sum(fetched, sent, 1, 2, 0)
    applied_own, applied_other, summed_own, summed_other = potentials((own, other), chosen)
    summed = [part[step] for part in (summed_own, summed_other) for step in range(STEPS)]
    transposed, back = ring_sum(summed, applied_other, 2, 1, 1)
    exchange = jnp.where(slab == 0, jnp.concatenate([applied_own, back]), jnp.concatenate([back, applied_own]))
    return exchange, transposed[0]


def broadcast(x, axis, root):
    mine = lax.axis_index(axis) == root
    return lax.psum(jnp.where(mine, x, jnp.zeros_like(x)), axis)


def frequency(counter, length):
    return jnp.where(counter <= length // 2, counter, counter - length).astype(jnp.float32)


def coulomb_kernel(freq_z, freq_y, freq_x):
    wave_first = 2.0 * math.pi / length_first
    wave_side = 2.0 * math.pi / length_side
    wave_last = 2.0 * math.pi / length_last
    squared = (
        (wave_first * freq_z)[:, None, None] ** 2
        + (wave_side * freq_y)[None, :, None] ** 2
        + (wave_last * freq_x)[None, None, :] ** 2
    )
    safe = jnp.where(squared > 0, squared, 1.0)
    screened = -4.0 * math.pi * jnp.expm1(-squared / (4.0 * omega_screen**2)) / safe
    return jnp.where(squared > 0, screened, math.pi / omega_screen**2)


def dft_table(length, direction):
    counter = jnp.arange(length)
    product = counter[:, None] * counter[None, :] % length
    angle = 2.0 * math.pi / length * product.astype(jnp.float32)
    return (jnp.cos(angle), direction * jnp.sin(angle))


def along_last(values, length, direction):
    cosines, sine_table = dft_table(length, direction)
    upper = jnp.concatenate([cosines, -sine_table], axis=1)
    lower = jnp.concatenate([sine_table, cosines], axis=1)
    matrix = jnp.concatenate([upper, lower], axis=0)
    return jnp.matmul(values, matrix, precision=lax.Precision.HIGHEST)


def along_axis(values, length, direction, pattern):
    cosines, sine_table = dft_table(length, direction)
    middle = values.shape[-1] // 2
    with_cos = jnp.einsum(pattern, cosines, values, precision=lax.Precision.HIGHEST)
    with_sin = jnp.einsum(pattern, sine_table, values, precision=lax.Precision.HIGHEST)
    real_part = with_cos[..., :middle] + with_sin[..., middle:]
    imag_part = with_cos[..., middle:] - with_sin[..., :middle]
    return jnp.concatenate([real_part, imag_part], axis=-1)


def per_device(orbitals, owner, picks):
    bloc, planes, points = orbitals.shape
    slab_count = lax.axis_size("slab")
    column_rows = NY // slab_count
    slab_index = lax.axis_index("slab")
    freq_y = frequency(slab_index * column_rows + jnp.arange(column_rows), NY)
    kernel = coulomb_kernel(frequency(jnp.arange(NZ), NZ), freq_y, frequency(jnp.arange(NX), NX))
    kernel = kernel * (1.0 / (NX * NY * NZ))
    kernel_tile = jnp.concatenate([kernel, kernel], axis=-1)
    exchange_sum = jnp.zeros_like(orbitals)
    collected = []
    for turn_index in range(STEPS):
        fetch_chosen = jnp.take(orbitals, picks[turn_index], axis=0)
        chosen = broadcast(fetch_chosen, "band", owner[turn_index])
        real_part = (orbitals * chosen[0]).reshape(bloc, planes, NY, NX)
        imag_part = (orbitals * chosen[1]).reshape(bloc, planes, NY, NX)
        fields = jnp.concatenate([real_part, imag_part], axis=-1)
        fields = along_last(fields, NX, 1.0)
        fields = along_axis(fields, NY, 1.0, "ky,bzyx->bzkx")
        columns = lax.all_to_all(fields, "slab", split_axis=2, concat_axis=1, tiled=True)
        columns = along_axis(columns, NZ, 1.0, "kz,bzyx->bkyx") * kernel_tile
        columns = along_axis(columns, NZ, -1.0, "kz,bzyx->bkyx")
        fields = lax.all_to_all(columns, "slab", split_axis=1, concat_axis=2, tiled=True)
        fields = along_axis(fields, NY, -1.0, "ky,bzyx->bzkx")
        fields = along_last(fields, NX, -1.0)
        count = fields.shape[0]
        potentials_first_part = fields[..., :NX].reshape(count, planes, points)
        potentials_second_part = fields[..., NX:].reshape(count, planes, points)
        applied = potentials_first_part * chosen[0] + potentials_second_part * chosen[1]
        contributions_local_sum = jnp.stack(
            [
                jnp.sum(potentials_first_part * orbitals, axis=0),
                jnp.sum(potentials_second_part * orbitals, axis=0),
            ]
        )
        applied, local_sum = (applied, contributions_local_sum)
        exchange_sum = exchange_sum + applied
        collected.append(lax.psum(local_sum, "band"))
    transposed = jnp.stack(collected)
    return (exchange_sum, transposed)


def solution(mesh):
    body = whole_bands if (mesh.shape["band"], mesh.shape["slab"]) == (2 * RING, 2) else per_device
    in_specs = (P("band", "slab", None), P(), P())
    out_specs = (P("band", "slab", None), P(None, None, "slab", None))
    return jax.shard_map(body, mesh=mesh, in_specs=in_specs, out_specs=out_specs, check_vma=False)
```

```python
import functools
import math

import jax
import jax.numpy as jnp
import numpy as np
from jax import lax
from jax.experimental import pallas as pl
from jax.experimental.pallas import tpu as pltpu
from jax.sharding import PartitionSpec as P

NX = 48
NY = 96
NZ = 96
STEPS = 2
OUTER = 12
INNER = 8
WIDE = INNER * NX
SIN60 = math.sqrt(3.0) / 2.0


length_first = 41.05
length_side = 41.05
length_last = 20.525
omega_screen = 0.106


def split_table(table):
    high = table.astype(jnp.bfloat16)
    low = (table - high.astype(np.float64)).astype(jnp.bfloat16)
    return high, low


def unit_table(rows, columns, length):
    angle = 2.0 * np.pi / length * (np.outer(rows, columns) % length)
    return np.cos(angle), np.sin(angle)


def plane_table():
    cy, sy = unit_table(np.arange(INNER), np.arange(INNER), INNER)
    cx, sx = unit_table(np.arange(NX), np.arange(NX), NX)
    cosines = np.kron(cy, cx) - np.kron(sy, sx)
    sines = np.kron(cy, sx) + np.kron(sy, cx)
    high, low = split_table(np.block([[cosines, -sines], [sines, cosines]]))
    return np.concatenate([high, high, low], axis=0)


def first_table(direction):
    cosines, sines = unit_table(np.arange(NZ), np.arange(NZ), NZ)
    sines = direction * sines
    high, low = split_table(np.block([[cosines, sines], [-sines, cosines]]))
    return np.concatenate([high, low, high], axis=1)


def twiddle_table():
    cosines, sines = unit_table(np.arange(OUTER), np.repeat(np.arange(INNER), NX), NY)
    return np.stack([cosines, sines]).astype(np.float32)


def screened_table():
    def signed(length):
        counter = np.arange(length)
        return np.where(counter <= length // 2, counter, counter - length).astype(np.float64)

    gz = 2.0 * math.pi / length_first * signed(NZ)
    gy = 2.0 * math.pi / length_side * signed(NY)
    gx = 2.0 * math.pi / length_last * signed(NX)
    squared = gz[:, None, None] ** 2 + gy[None, :, None] ** 2 + gx[None, None, :] ** 2
    safe = np.where(squared > 0, squared, 1.0)
    screened = -4.0 * math.pi * np.expm1(-squared / (4.0 * omega_screen**2)) / safe
    kernel = np.where(squared > 0, screened, math.pi / omega_screen**2) / (NX * NY * NZ)
    kernel = kernel.reshape(NZ, INNER, OUTER, NX).transpose(2, 0, 1, 3)
    return kernel.reshape(OUTER * NZ, WIDE).astype(np.float32)


def transform3(parts):
    (r0, i0), (r1, i1), (r2, i2) = parts
    sr, si = r1 + r2, i1 + i2
    dr, di = SIN60 * (r1 - r2), SIN60 * (i1 - i2)
    mr, mi = r0 - 0.5 * sr, i0 - 0.5 * si
    return [(r0 + sr, i0 + si), (mr + di, mi - dr), (mr - di, mi + dr)]


def transform4(parts):
    (r0, i0), (r1, i1), (r2, i2), (r3, i3) = parts
    ar, ai, br, bi = r0 + r2, i0 + i2, r0 - r2, i0 - i2
    cr, ci, dr, di = r1 + r3, i1 + i3, r1 - r3, i1 - i3
    return [(ar + cr, ai + ci), (br + di, bi - dr), (ar - cr, ai - ci), (br - di, bi + dr)]


def transform12(values):
    rows = []
    for n2 in range(4):
        rows.append(transform3([values[(4 * n1 + 3 * n2) % 12] for n1 in range(3)]))
    out = [None] * 12
    for k1 in range(3):
        column = transform4([rows[n2][k1] for n2 in range(4)])
        for k2 in range(4):
            out[(4 * k1 + 9 * k2) % 12] = column[k2]
    return out


def swapped(values):
    return [(im, re) for re, im in values]


def halves(value):
    high = value.astype(jnp.bfloat16)
    return high, (value - high.astype(jnp.float32)).astype(jnp.bfloat16)


def put(split_ref, rows, column, value):
    high, low = halves(value)
    width = value.shape[-1]
    split_ref[rows, pl.ds(column, width)] = high
    split_ref[rows, pl.ds(2 * WIDE + column, width)] = low
    split_ref[rows, pl.ds(4 * WIDE + column, width)] = high


def potential_stages(tables, orbital_refs, chosen_ref, previous_refs, applied_refs, summed_refs, split_ref, field_ref):
    plane_ref, forth_ref, back_ref, twiddle_ref, screen_ref = tables
    bands, planes, _ = orbital_refs[0].shape
    tall = 16

    def pair_fields(band, part, lane):
        @pl.loop(0, planes // tall)
        def _(step):
            start = pl.multiple_of(step * tall, tall)
            here = pl.ds(start, tall)
            values = []
            for outer in range(OUTER):
                cols = pl.ds(outer * WIDE + lane, 128)
                orbital = orbital_refs[part][band, here, cols]
                values.append((orbital * chosen_ref[part, 0, here, cols], orbital * chosen_ref[part, 1, here, cols]))
            for k1, (re, im) in enumerate(transform12(values)):
                if k1:
                    tc = twiddle_ref[0, pl.ds(k1, 1), pl.ds(lane, 128)]
                    ts = twiddle_ref[1, pl.ds(k1, 1), pl.ds(lane, 128)]
                    re, im = re * tc + im * ts, im * tc - re * ts
                rows = pl.ds(pl.multiple_of(k1 * NZ + part * planes + start, tall), tall)
                put(split_ref, rows, lane, re)
                put(split_ref, rows, WIDE + lane, im)

    def plane_pass():
        chunk = 384

        @pl.loop(0, OUTER * NZ // chunk)
        def _(step):
            rows = pl.ds(pl.multiple_of(step * chunk, chunk), chunk)
            field_ref[rows, :] = jnp.dot(split_ref[rows, :], plane_ref[...], preferred_element_type=jnp.float32)

    def screen_columns(first, last):
        @pl.loop(first, last)
        def _(k1):
            rows = pl.ds(pl.multiple_of(k1 * NZ, NZ), NZ)
            field = jnp.concatenate([field_ref[rows, :WIDE], field_ref[rows, WIDE:]], axis=0)
            high, low = halves(field)
            field = jnp.dot(forth_ref[...], jnp.concatenate([high, high, low], axis=0), preferred_element_type=jnp.float32)
            screen = screen_ref[rows, :]
            field = field * jnp.concatenate([screen, screen], axis=0)
            high, low = halves(field)
            field = jnp.dot(back_ref[...], jnp.concatenate([high, high, low], axis=0), preferred_element_type=jnp.float32)
            put(split_ref, rows, 0, field[NZ:])
            put(split_ref, rows, WIDE, field[:NZ])

    def apply(band, part, lane):
        @pl.loop(0, planes // 8)
        def _(step):
            start = pl.multiple_of(step * 8, 8)
            here = pl.ds(start, 8)
            values = []
            for k1 in range(OUTER):
                rows = pl.ds(pl.multiple_of(k1 * NZ + part * planes + start, 8), 8)
                im = field_ref[rows, pl.ds(lane, 128)]
                re = field_ref[rows, pl.ds(WIDE + lane, 128)]
                if k1:
                    tc = twiddle_ref[0, pl.ds(k1, 1), pl.ds(lane, 128)]
                    ts = twiddle_ref[1, pl.ds(k1, 1), pl.ds(lane, 128)]
                    re, im = re * tc - im * ts, re * ts + im * tc
                values.append((re, im))
            for outer, (first, second) in enumerate(swapped(transform12(swapped(values)))):
                cols = pl.ds(outer * WIDE + lane, 128)
                orbital = orbital_refs[part][band, here, cols]
                applied = first * chosen_ref[part, 0, here, cols] + second * chosen_ref[part, 1, here, cols]
                if previous_refs:
                    applied = applied + previous_refs[part][band, here, cols]
                applied_refs[part][band, here, cols] = applied
                first, second = first * orbital, second * orbital
                if band:
                    first = first + summed_refs[part][0, here, cols]
                    second = second + summed_refs[part][1, here, cols]
                summed_refs[part][0, here, cols] = first
                summed_refs[part][1, here, cols] = second

    for band in range(bands):
        for lane in range(0, WIDE, 128):
            pair_fields(band, 0, lane)
            pair_fields(band, 1, lane)
            yield
        plane_pass()
        yield
        for first in range(0, OUTER, 4):
            screen_columns(first, first + 4)
            yield
        plane_pass()
        yield
        for lane in range(0, WIDE, 128):
            apply(band, 0, lane)
            apply(band, 1, lane)
            yield


RING = 8
BLOCKS = 4


def ring_band(position, core):
    x = position // 4
    z = x * (7 - 2 * position) + position
    return (z * 2 + x) * 2 + core


def way_lanes(width):
    first = (width // 128 + 1) // 2 * 128
    return (0, first), (first, width - first)


def ring_stages(inputs, parcel_ref, out_ref, got_ref, scratch):
    twin_ref, total_ref, ring_ref, cross_ref = scratch[:4]
    twin_send, twin_recv, ring_send, ring_recv, lone_send, lone_recv, gather_send, gather_recv, hand_send, hand_recv = scratch[4:]
    slabs_in, slabs_out = len(inputs), out_ref.shape[0]
    planes, points = inputs[0].shape[-2:]
    half, width = planes // 2, points // BLOCKS
    band, slab = lax.axis_index("band"), lax.axis_index("slab")
    core, x, z = band % 2, (band // 2) % 2, band // 4
    place = x * (7 - 2 * z) + z
    twin = {"band": band + 1 - 2 * core}
    across = {"slab": 1 - slab}
    ends = [{"band": ring_band((place + 1) % RING, core)}, {"band": ring_band((place + RING - 1) % RING, core)}]

    barrier = pltpu.get_barrier_semaphore()
    for device in [twin, across] + ends:
        pl.semaphore_signal(barrier, inc=1, device_id=device, device_id_type=pl.DeviceIdType.MESH)
    pl.semaphore_wait(barrier, 4)

    def push(source, target, send, recv, device):
        copy = pltpu.make_async_remote_copy(
            src_ref=source,
            dst_ref=target,
            send_sem=send,
            recv_sem=recv,
            device_id=device,
            device_id_type=pl.DeviceIdType.MESH,
        )
        copy.start()
        return copy

    def spot(chunk, way):
        offset, extent = way_lanes(width)[way]
        lanes = pl.ds(pl.multiple_of((chunk % BLOCKS) * width + offset, 128), extent)
        return pl.ds(pl.multiple_of(chunk // BLOCKS * half, 8), half), lanes

    parcel = None
    if parcel_ref is not None:
        parcel = push(parcel_ref, got_ref, lone_send.at[0], lone_recv.at[0], across)

    swaps = []
    for at, ref in enumerate(inputs):
        swaps.append(push(ref.at[1 - core], twin_ref.at[at], twin_send.at[at], twin_recv.at[at], twin))
    yield
    for at, ref in enumerate(inputs):
        swaps[at].wait_recv()
        total_ref[at] = ref[core] + twin_ref[at]

    hops = []
    for hop in range(RING - 1):
        for way in range(2):
            sign = 1 - 2 * way
            chunk = (place + sign * (-1 - hop) + 2 * RING) % RING
            rows, lanes = spot(chunk, way)
            extent = way_lanes(width)[way][1]
            source = total_ref.at[:, rows, lanes]
            if hop:
                hops[-2].wait_recv()
                arrived = ring_ref.at[way, hop - 1, :, :, pl.ds(0, extent)]
                arrived[...] += total_ref[:, rows, lanes]
                source = arrived
            target = ring_ref.at[way, hop, :, :, pl.ds(0, extent)]
            hops.append(push(source, target, ring_send.at[way, hop], ring_recv.at[way, hop], ends[way]))
        yield
    for way in range(2):
        hops[-2 + way].wait_recv()
        rows, lanes = spot(place, way)
        offset, extent = way_lanes(width)[way]
        done = ring_ref[way, RING - 2, :, :, pl.ds(0, extent)] + total_ref[:, rows, lanes]
        out_ref[0, core, rows, lanes] = done[0]
        if slabs_in == 2:
            cross_ref[0, :, pl.ds(offset, extent)] = done[1]
    rows, _ = spot(place, 0)
    lanes = pl.ds(pl.multiple_of(place % BLOCKS * width, 128), width)
    own = out_ref.at[0, core, rows, lanes]
    if slabs_in == 2:
        crossing = push(cross_ref.at[0], cross_ref.at[1], lone_send.at[1], lone_recv.at[1], across)
        yield
        crossing.wait_recv()
        own[...] += cross_ref[1]
    else:
        crossing = push(own, out_ref.at[1, core, rows, lanes], lone_send.at[1], lone_recv.at[1], across)

    hands = []
    last = {}
    for hop in range(RING):
        for part in range(slabs_out):
            if hop == 0 and part == 1:
                yield
                crossing.wait_recv()
            for way in range(2):
                sign = 1 - 2 * way
                rows, lanes = spot((place - sign * hop + RING) % RING, way)
                if hop:
                    last[part, way].wait_recv()
                here = out_ref.at[part, core, rows, lanes]
                if hop < RING - 1:
                    copy = push(here, here, gather_send.at[part, way, hop], gather_recv.at[part, way, hop], ends[way])
                    last[part, way] = copy
                    hops.append(copy)
                hands.append(push(here, here, hand_send.at[part, way, hop], hand_recv.at[part, way, hop], twin))
        yield
    for copy in swaps + hops + [crossing]:
        copy.wait_send()
    for copy in hands:
        copy.wait()
    if parcel is not None:
        parcel.wait()


def step_kernel(counts, *refs):
    refs = list(refs)
    groups = []
    for count in counts:
        groups.append(refs[:count])
        refs = refs[count:]
    tables, orbitals, chosen, previous, inputs, parcel, applied, summed, out, got, fields, scratch = groups
    ring = iter(()) if not inputs else ring_stages(inputs, parcel[0] if parcel else None, out[0], got[0] if got else None, scratch)
    if tables:
        for _ in potential_stages(tables, orbitals, chosen[0], previous, applied, summed, *fields):
            next(ring, None)
    for _ in ring:
        pass


def run_step(collective, orbitals=(), chosen=(), previous=(), inputs=(), parcel=()):
    planes, points = (list(inputs) + list(orbitals))[0].shape[-2:]
    half, width = planes // 2, points // BLOCKS
    slabs_in = len(inputs)
    slabs_out = 3 - slabs_in
    rows = OUTER * NZ
    dma = pltpu.SemaphoreType.DMA
    vmem = pl.BlockSpec(memory_space=pltpu.VMEM)
    anywhere = pl.BlockSpec(memory_space=pl.ANY)
    tables, shapes, fields, ring, flops = [], [], [], [], 0
    pair = jax.ShapeDtypeStruct((2, planes, points), jnp.float32)
    if orbitals:
        tables = [plane_table(), first_table(1.0), first_table(-1.0), twiddle_table(), screened_table()]
        tables = [jnp.asarray(table) for table in tables]
        shapes = [jax.ShapeDtypeStruct(part.shape, jnp.float32) for part in orbitals] + [pair] * 2
        fields = [pltpu.VMEM((rows, 6 * WIDE), jnp.bfloat16), pltpu.VMEM((rows, 2 * WIDE), jnp.float32)]
        flops = 2 * (2 * 2 * rows * 6 * WIDE * 2 * WIDE + 2 * 2 * 2 * NZ * 6 * NZ * OUTER * WIDE)
    specs = [vmem] * len(shapes)
    if inputs:
        shapes.append(jax.ShapeDtypeStruct((slabs_out, 2, planes, points), jnp.float32))
        specs.append(vmem)
        ring = [
            pltpu.VMEM((slabs_in, planes, points), jnp.float32),
            pltpu.VMEM((slabs_in, planes, points), jnp.float32),
            pltpu.VMEM((2, RING - 1, slabs_in, half, way_lanes(width)[0][1]), jnp.float32),
            pltpu.VMEM((2, half, width), jnp.float32),
            dma((slabs_in,)),
            dma((slabs_in,)),
            dma((2, RING - 1)),
            dma((2, RING - 1)),
            dma((2,)),
            dma((2,)),
            dma((slabs_out, 2, RING - 1)),
            dma((slabs_out, 2, RING - 1)),
            dma((slabs_out, 2, RING)),
            dma((slabs_out, 2, RING)),
        ]
    for part in parcel:
        shapes.append(jax.ShapeDtypeStruct(part.shape, jnp.float32))
        specs.append(anywhere)
    operands = [tables, orbitals, chosen, previous, inputs, parcel]
    counts = [len(group) for group in operands]
    counts += [len(orbitals), 2 if orbitals else 0, 1 if inputs else 0, len(parcel), len(fields), len(ring)]
    operands = [array for group in operands for array in group]
    return pl.pallas_call(
        functools.partial(step_kernel, tuple(counts)),
        out_shape=shapes,
        in_specs=[vmem] * (len(operands) - len(parcel)) + [anywhere] * len(parcel),
        out_specs=specs,
        scratch_shapes=fields + ring,
        compiler_params=pltpu.CompilerParams(
            collective_id=collective, has_side_effects=True, vmem_limit_bytes=56 * 1024 * 1024
        ),
        cost_estimate=pl.CostEstimate(flops=flops, bytes_accessed=20 * planes * points * 4, transcendentals=0),
    )(*operands)


def whole_bands(orbitals, owner, picks):
    bloc, planes, points = orbitals.shape
    half = bloc // 2
    slab = lax.axis_index("slab")
    band = lax.axis_index("band")
    fetched = []
    for step in range(STEPS):
        rows = jnp.stack([lax.dynamic_index_in_dim(orbitals, picks[step, row], 0, keepdims=False) for row in range(2)])
        fetched.append(jnp.where(band == owner[step], rows, jnp.zeros_like(rows)))
    own = lax.dynamic_slice_in_dim(orbitals, slab * half, half, 0)
    sent = lax.dynamic_slice_in_dim(orbitals, (1 - slab) * half, half, 0)
    chosen, other = run_step(0, inputs=fetched[:1], parcel=[sent])
    parts = [own, other]
    *applied, summed_own, summed_other, chosen = run_step(1, parts, [chosen], inputs=fetched[1:])
    *applied, late_own, late_other, early = run_step(2, parts, [chosen], applied, [summed_own, summed_other])
    late, back = run_step(3, inputs=[late_own, late_other], parcel=applied[1:])
    exchange = jnp.where(slab == 0, jnp.concatenate([applied[0], back]), jnp.concatenate([back, applied[0]]))
    return exchange, jnp.concatenate([early, late])


def broadcast(x, axis, root):
    mine = lax.axis_index(axis) == root
    return lax.psum(jnp.where(mine, x, jnp.zeros_like(x)), axis)


def frequency(counter, length):
    return jnp.where(counter <= length // 2, counter, counter - length).astype(jnp.float32)


def coulomb_kernel(freq_z, freq_y, freq_x):
    wave_first = 2.0 * math.pi / length_first
    wave_side = 2.0 * math.pi / length_side
    wave_last = 2.0 * math.pi / length_last
    squared = (
        (wave_first * freq_z)[:, None, None] ** 2
        + (wave_side * freq_y)[None, :, None] ** 2
        + (wave_last * freq_x)[None, None, :] ** 2
    )
    safe = jnp.where(squared > 0, squared, 1.0)
    screened = -4.0 * math.pi * jnp.expm1(-squared / (4.0 * omega_screen**2)) / safe
    return jnp.where(squared > 0, screened, math.pi / omega_screen**2)


def dft_table(length, direction):
    counter = jnp.arange(length)
    product = counter[:, None] * counter[None, :] % length
    angle = 2.0 * math.pi / length * product.astype(jnp.float32)
    return (jnp.cos(angle), direction * jnp.sin(angle))


def along_last(values, length, direction):
    cosines, sine_table = dft_table(length, direction)
    upper = jnp.concatenate([cosines, -sine_table], axis=1)
    lower = jnp.concatenate([sine_table, cosines], axis=1)
    matrix = jnp.concatenate([upper, lower], axis=0)
    return jnp.matmul(values, matrix, precision=lax.Precision.HIGHEST)


def along_axis(values, length, direction, pattern):
    cosines, sine_table = dft_table(length, direction)
    middle = values.shape[-1] // 2
    with_cos = jnp.einsum(pattern, cosines, values, precision=lax.Precision.HIGHEST)
    with_sin = jnp.einsum(pattern, sine_table, values, precision=lax.Precision.HIGHEST)
    real_part = with_cos[..., :middle] + with_sin[..., middle:]
    imag_part = with_cos[..., middle:] - with_sin[..., :middle]
    return jnp.concatenate([real_part, imag_part], axis=-1)


def per_device(orbitals, owner, picks):
    bloc, planes, points = orbitals.shape
    slab_count = lax.axis_size("slab")
    column_rows = NY // slab_count
    slab_index = lax.axis_index("slab")
    freq_y = frequency(slab_index * column_rows + jnp.arange(column_rows), NY)
    kernel = coulomb_kernel(frequency(jnp.arange(NZ), NZ), freq_y, frequency(jnp.arange(NX), NX))
    kernel = kernel * (1.0 / (NX * NY * NZ))
    kernel_tile = jnp.concatenate([kernel, kernel], axis=-1)
    exchange_sum = jnp.zeros_like(orbitals)
    collected = []
    for turn_index in range(STEPS):
        fetch_chosen = jnp.take(orbitals, picks[turn_index], axis=0)
        chosen = broadcast(fetch_chosen, "band", owner[turn_index])
        real_part = (orbitals * chosen[0]).reshape(bloc, planes, NY, NX)
        imag_part = (orbitals * chosen[1]).reshape(bloc, planes, NY, NX)
        fields = jnp.concatenate([real_part, imag_part], axis=-1)
        fields = along_last(fields, NX, 1.0)
        fields = along_axis(fields, NY, 1.0, "ky,bzyx->bzkx")
        columns = lax.all_to_all(fields, "slab", split_axis=2, concat_axis=1, tiled=True)
        columns = along_axis(columns, NZ, 1.0, "kz,bzyx->bkyx") * kernel_tile
        columns = along_axis(columns, NZ, -1.0, "kz,bzyx->bkyx")
        fields = lax.all_to_all(columns, "slab", split_axis=1, concat_axis=2, tiled=True)
        fields = along_axis(fields, NY, -1.0, "ky,bzyx->bzkx")
        fields = along_last(fields, NX, -1.0)
        count = fields.shape[0]
        potentials_first_part = fields[..., :NX].reshape(count, planes, points)
        potentials_second_part = fields[..., NX:].reshape(count, planes, points)
        applied = potentials_first_part * chosen[0] + potentials_second_part * chosen[1]
        contributions_local_sum = jnp.stack(
            [
                jnp.sum(potentials_first_part * orbitals, axis=0),
                jnp.sum(potentials_second_part * orbitals, axis=0),
            ]
        )
        applied, local_sum = (applied, contributions_local_sum)
        exchange_sum = exchange_sum + applied
        collected.append(lax.psum(local_sum, "band"))
    transposed = jnp.stack(collected)
    return (exchange_sum, transposed)


def solution(mesh):
    body = whole_bands if (mesh.shape["band"], mesh.shape["slab"]) == (2 * RING, 2) else per_device
    in_specs = (P("band", "slab", None), P(), P())
    out_specs = (P("band", "slab", None), P(None, None, "slab", None))
    return jax.shard_map(body, mesh=mesh, in_specs=in_specs, out_specs=out_specs, check_vma=False)
```

```python
import functools
import math

import jax
import jax.numpy as jnp
import numpy as np
from jax import lax
from jax.experimental import pallas as pl
from jax.experimental.pallas import tpu as pltpu
from jax.sharding import PartitionSpec as P

NX = 48
NY = 96
NZ = 96
STEPS = 2
OUTER = 12
INNER = 8
WIDE = INNER * NX
SIN60 = math.sqrt(3.0) / 2.0


length_first = 41.05
length_side = 41.05
length_last = 20.525
omega_screen = 0.106


def split_table(table):
    high = table.astype(jnp.bfloat16)
    low = (table - high.astype(np.float64)).astype(jnp.bfloat16)
    return high, low


def unit_table(rows, columns, length):
    angle = 2.0 * np.pi / length * (np.outer(rows, columns) % length)
    return np.cos(angle), np.sin(angle)


def plane_table():
    cy, sy = unit_table(np.arange(INNER), np.arange(INNER), INNER)
    cx, sx = unit_table(np.arange(NX), np.arange(NX), NX)
    cosines = np.kron(cy, cx) - np.kron(sy, sx)
    sines = np.kron(cy, sx) + np.kron(sy, cx)
    high, low = split_table(np.block([[cosines, -sines], [sines, cosines]]))
    return np.concatenate([high, high, low], axis=0)


def first_table(direction):
    cosines, sines = unit_table(np.arange(NZ), np.arange(NZ), NZ)
    sines = direction * sines
    high, low = split_table(np.block([[cosines, sines], [-sines, cosines]]))
    return np.concatenate([high, low, high], axis=1)


def twiddle_table():
    cosines, sines = unit_table(np.arange(OUTER), np.repeat(np.arange(INNER), NX), NY)
    return np.stack([cosines, sines]).astype(np.float32)


def screened_table():
    def signed(length):
        counter = np.arange(length)
        return np.where(counter <= length // 2, counter, counter - length).astype(np.float64)

    gz = 2.0 * math.pi / length_first * signed(NZ)
    gy = 2.0 * math.pi / length_side * signed(NY)
    gx = 2.0 * math.pi / length_last * signed(NX)
    squared = gz[:, None, None] ** 2 + gy[None, :, None] ** 2 + gx[None, None, :] ** 2
    safe = np.where(squared > 0, squared, 1.0)
    screened = -4.0 * math.pi * np.expm1(-squared / (4.0 * omega_screen**2)) / safe
    kernel = np.where(squared > 0, screened, math.pi / omega_screen**2) / (NX * NY * NZ)
    kernel = kernel.reshape(NZ, INNER, OUTER, NX).transpose(2, 0, 1, 3)
    return kernel.reshape(OUTER * NZ, WIDE).astype(np.float32)


def transform3(parts):
    (r0, i0), (r1, i1), (r2, i2) = parts
    sr, si = r1 + r2, i1 + i2
    dr, di = SIN60 * (r1 - r2), SIN60 * (i1 - i2)
    mr, mi = r0 - 0.5 * sr, i0 - 0.5 * si
    return [(r0 + sr, i0 + si), (mr + di, mi - dr), (mr - di, mi + dr)]


def transform4(parts):
    (r0, i0), (r1, i1), (r2, i2), (r3, i3) = parts
    ar, ai, br, bi = r0 + r2, i0 + i2, r0 - r2, i0 - i2
    cr, ci, dr, di = r1 + r3, i1 + i3, r1 - r3, i1 - i3
    return [(ar + cr, ai + ci), (br + di, bi - dr), (ar - cr, ai - ci), (br - di, bi + dr)]


def transform12(values):
    rows = []
    for n2 in range(4):
        rows.append(transform3([values[(4 * n1 + 3 * n2) % 12] for n1 in range(3)]))
    out = [None] * 12
    for k1 in range(3):
        column = transform4([rows[n2][k1] for n2 in range(4)])
        for k2 in range(4):
            out[(4 * k1 + 9 * k2) % 12] = column[k2]
    return out


def swapped(values):
    return [(im, re) for re, im in values]


def halves(value):
    high = value.astype(jnp.bfloat16)
    return high, (value - high.astype(jnp.float32)).astype(jnp.bfloat16)


def put(split_ref, rows, column, value):
    high, low = halves(value)
    width = value.shape[-1]
    split_ref[rows, pl.ds(column, width)] = high
    split_ref[rows, pl.ds(2 * WIDE + column, width)] = low
    split_ref[rows, pl.ds(4 * WIDE + column, width)] = high


def potential_kernel(*refs):
    plane_ref, forth_ref, back_ref, twiddle_ref, screen_ref = refs[:5]
    orbital_refs, chosen_refs = refs[5:7], refs[7:9]
    applied_refs, summed_refs = refs[9:11], refs[11:13]
    split_ref, field_ref = refs[13:15]
    turn = pl.program_id(1)
    planes = orbital_refs[0].shape[1]
    tall = 16

    for part in range(2):
        for lane in range(0, WIDE, 128):

            @pl.loop(0, planes // tall)
            def _(step, part=part, lane=lane):
                start = pl.multiple_of(step * tall, tall)
                here = pl.ds(start, tall)
                values = []
                for outer in range(OUTER):
                    cols = pl.ds(outer * WIDE + lane, 128)
                    orbital = orbital_refs[part][0, here, cols]
                    values.append((orbital * chosen_refs[part][0, 0, 0, here, cols], orbital * chosen_refs[part][0, 0, 1, here, cols]))
                for k1, (re, im) in enumerate(transform12(values)):
                    if k1:
                        tc = twiddle_ref[0, pl.ds(k1, 1), pl.ds(lane, 128)]
                        ts = twiddle_ref[1, pl.ds(k1, 1), pl.ds(lane, 128)]
                        re, im = re * tc + im * ts, im * tc - re * ts
                    rows = pl.ds(pl.multiple_of(k1 * NZ + part * planes + start, tall), tall)
                    put(split_ref, rows, lane, re)
                    put(split_ref, rows, WIDE + lane, im)

    def plane_pass():
        chunk = 384

        @pl.loop(0, OUTER * NZ // chunk)
        def _(step):
            rows = pl.ds(pl.multiple_of(step * chunk, chunk), chunk)
            field_ref[rows, :] = jnp.dot(split_ref[rows, :], plane_ref[...], preferred_element_type=jnp.float32)

    plane_pass()

    @pl.loop(0, OUTER)
    def _(k1):
        rows = pl.ds(pl.multiple_of(k1 * NZ, NZ), NZ)
        field = jnp.concatenate([field_ref[rows, :WIDE], field_ref[rows, WIDE:]], axis=0)
        high, low = halves(field)
        field = jnp.dot(forth_ref[...], jnp.concatenate([high, high, low], axis=0), preferred_element_type=jnp.float32)
        screen = screen_ref[rows, :]
        field = field * jnp.concatenate([screen, screen], axis=0)
        high, low = halves(field)
        field = jnp.dot(back_ref[...], jnp.concatenate([high, high, low], axis=0), preferred_element_type=jnp.float32)
        put(split_ref, rows, 0, field[NZ:])
        put(split_ref, rows, WIDE, field[:NZ])

    plane_pass()

    @pl.when(pl.program_id(0) == 0)
    def _():
        for summed_ref in summed_refs:
            summed_ref[turn] = jnp.zeros(summed_ref.shape[1:], jnp.float32)

    for part in range(2):
        for lane in range(0, WIDE, 128):

            @pl.loop(0, planes // 8)
            def _(step, part=part, lane=lane):
                start = pl.multiple_of(step * 8, 8)
                here = pl.ds(start, 8)
                values = []
                for k1 in range(OUTER):
                    rows = pl.ds(pl.multiple_of(k1 * NZ + part * planes + start, 8), 8)
                    im = field_ref[rows, pl.ds(lane, 128)]
                    re = field_ref[rows, pl.ds(WIDE + lane, 128)]
                    if k1:
                        tc = twiddle_ref[0, pl.ds(k1, 1), pl.ds(lane, 128)]
                        ts = twiddle_ref[1, pl.ds(k1, 1), pl.ds(lane, 128)]
                        re, im = re * tc - im * ts, re * ts + im * tc
                    values.append((re, im))
                for outer, (first, second) in enumerate(swapped(transform12(swapped(values)))):
                    cols = pl.ds(outer * WIDE + lane, 128)
                    orbital = orbital_refs[part][0, here, cols]
                    applied = first * chosen_refs[part][0, 0, 0, here, cols] + second * chosen_refs[part][0, 0, 1, here, cols]
                    before = applied_refs[part][0, here, cols]
                    applied_refs[part][0, here, cols] = jnp.where(turn == 0, applied, applied + before)
                    summed_refs[part][turn, 0, here, cols] += first * orbital
                    summed_refs[part][turn, 1, here, cols] += second * orbital


def potentials(orbital_parts, chosen):
    count, planes, points = orbital_parts[0].shape
    tables = [plane_table(), first_table(1.0), first_table(-1.0), twiddle_table(), screened_table()]
    tables = [jnp.asarray(table) for table in tables]

    def constant(shape, **mode):
        return pl.BlockSpec(shape, lambda band, turn: (0,) * len(shape), **mode)

    def chosen_part(part):
        return pl.BlockSpec((1, 1, 2, planes, points), lambda band, turn: (part, turn, 0, 0, 0))

    per_band = pl.BlockSpec((1, planes, points), lambda band, turn: (band, 0, 0))
    summed = (STEPS, 2, planes, points)
    band_shape = jax.ShapeDtypeStruct((count, planes, points), jnp.float32)
    rows = OUTER * NZ
    flops = STEPS * count * (2 * 2 * rows * 6 * WIDE * 2 * WIDE + 2 * 2 * 2 * NZ * 6 * NZ * OUTER * WIDE)
    return pl.pallas_call(
        potential_kernel,
        grid=(count, STEPS),
        out_shape=[band_shape] * 2 + [jax.ShapeDtypeStruct(summed, jnp.float32)] * 2,
        in_specs=[constant(table.shape, pipeline_mode=pl.Buffered(1)) for table in tables]
        + [per_band] * 2
        + [chosen_part(0), chosen_part(1)],
        out_specs=[per_band] * 2 + [constant(summed)] * 2,
        scratch_shapes=[
            pltpu.VMEM((rows, 6 * WIDE), jnp.bfloat16),
            pltpu.VMEM((rows, 2 * WIDE), jnp.float32),
        ],
        compiler_params=pltpu.CompilerParams(
            vmem_limit_bytes=56 * 1024 * 1024, dimension_semantics=("arbitrary", "arbitrary")
        ),
        cost_estimate=pl.CostEstimate(flops=flops, bytes_accessed=4 * planes * points * 32, transcendentals=0),
    )(*tables, *orbital_parts, chosen, chosen)


RING = 8
BLOCKS = 4


def ring_band(position, core):
    x = position // 4
    z = x * (7 - 2 * position) + position
    return (z * 2 + x) * 2 + core


def ring_kernel(slabs_in, slabs_out, *refs):
    inputs = refs[: slabs_in * STEPS]
    parcel_ref, out_ref, got_ref = refs[slabs_in * STEPS : slabs_in * STEPS + 3]
    twin_ref, total_ref, ring_ref, cross_ref = refs[slabs_in * STEPS + 3 : slabs_in * STEPS + 7]
    twin_send, twin_recv, ring_send, ring_recv, lone_send, lone_recv, gather_send, gather_recv, hand_send, hand_recv = refs[
        slabs_in * STEPS + 7 :
    ]
    planes, points = inputs[0].shape[-2:]
    half, width = planes // 2, points // BLOCKS
    band, slab = lax.axis_index("band"), lax.axis_index("slab")
    core, x, z = band % 2, (band // 2) % 2, band // 4
    place = x * (7 - 2 * z) + z
    twin = {"band": band + 1 - 2 * core}
    across = {"slab": 1 - slab}
    ends = [{"band": ring_band((place + 1) % RING, core)}, {"band": ring_band((place + RING - 1) % RING, core)}]

    barrier = pltpu.get_barrier_semaphore()
    for device in [twin, across] + ends:
        pl.semaphore_signal(barrier, inc=1, device_id=device, device_id_type=pl.DeviceIdType.MESH)
    pl.semaphore_wait(barrier, 4)

    def push(source, target, send, recv, device):
        copy = pltpu.make_async_remote_copy(
            src_ref=source,
            dst_ref=target,
            send_sem=send,
            recv_sem=recv,
            device_id=device,
            device_id_type=pl.DeviceIdType.MESH,
        )
        copy.start()
        return copy

    def spot(chunk, way):
        lanes = pl.ds(pl.multiple_of((chunk % BLOCKS) * width, 128), width)
        return chunk // BLOCKS, pl.ds(way * half, half), lanes

    parcels = [push(parcel_ref.at[0], got_ref.at[0], lone_send.at[0], lone_recv.at[0], across)]

    swaps = []
    for at, ref in enumerate(inputs):
        swaps.append(push(ref.at[1 - core], twin_ref.at[at], twin_send.at[at], twin_recv.at[at], twin))
    for at, ref in enumerate(inputs):
        swaps[at].wait_recv()
        total_ref[at // STEPS, at % STEPS] = ref[core] + twin_ref[at]

    hops = []
    for hop in range(RING - 1):
        for way in range(2):
            sign = 1 - 2 * way
            chunk = (place + sign * (-1 - hop) + 2 * RING) % RING
            step, rows, lanes = spot(chunk, way)
            source = total_ref.at[:, step, rows, lanes]
            if hop:
                hops[-2].wait_recv()
                arrived = ring_ref.at[way, hop - 1]
                arrived[...] += total_ref[:, step, rows, lanes]
                source = arrived
            hops.append(push(source, ring_ref.at[way, hop], ring_send.at[way, hop], ring_recv.at[way, hop], ends[way]))
    step, _, lanes = spot(place, 0)
    for way in range(2):
        hops[-2 + way].wait_recv()
        _, rows, _ = spot(place, way)
        done = ring_ref[way, RING - 2] + total_ref[:, step, rows, lanes]
        out_ref[0, step, core, rows, lanes] = done[0]
        if slabs_in == 2:
            cross_ref[0, rows, :] = done[1]
    if slabs_in == 2:
        crossing = push(cross_ref.at[0], cross_ref.at[1], lone_send.at[1], lone_recv.at[1], across)
        parcels.append(push(parcel_ref.at[1], got_ref.at[1], lone_send.at[2], lone_recv.at[2], across))
        crossing.wait_recv()
        out_ref[0, step, core, :, lanes] += cross_ref[1]
    else:
        own = out_ref.at[0, step, core, :, lanes]
        crossing = push(own, out_ref.at[1, step, core, :, lanes], lone_send.at[1], lone_recv.at[1], across)
        parcels.append(push(parcel_ref.at[1], got_ref.at[1], lone_send.at[2], lone_recv.at[2], across))

    hands = []
    last = {}
    for hop in range(RING):
        for part in range(slabs_out):
            if hop == 0 and part == 1:
                crossing.wait_recv()
            for way in range(2):
                sign = 1 - 2 * way
                step, rows, lanes = spot((place - sign * hop + RING) % RING, way)
                if hop:
                    last[part, way].wait_recv()
                here = out_ref.at[part, step, core, rows, lanes]
                if hop < RING - 1:
                    copy = push(here, here, gather_send.at[part, way, hop], gather_recv.at[part, way, hop], ends[way])
                    last[part, way] = copy
                    hops.append(copy)
                hands.append(push(here, here, hand_send.at[part, way, hop], hand_recv.at[part, way, hop], twin))
    for copy in swaps + hops:
        copy.wait_send()
    crossing.wait_send()
    for copy in hands:
        copy.wait()
    for copy in parcels:
        copy.wait()


def ring_sum(inputs, parcel, slabs_in, slabs_out, collective):
    planes, points = inputs[0].shape[-2:]
    half, width = planes // 2, points // BLOCKS
    dma = pltpu.SemaphoreType.DMA
    vmem = pl.BlockSpec(memory_space=pltpu.VMEM)
    anywhere = pl.BlockSpec(memory_space=pl.ANY)
    out = jax.ShapeDtypeStruct((slabs_out, STEPS, 2, planes, points), jnp.float32)
    return pl.pallas_call(
        functools.partial(ring_kernel, slabs_in, slabs_out),
        out_shape=[out, jax.ShapeDtypeStruct(parcel.shape, jnp.float32)],
        in_specs=[vmem] * len(inputs) + [anywhere],
        out_specs=[vmem, anywhere],
        scratch_shapes=[
            pltpu.VMEM((len(inputs), planes, points), jnp.float32),
            pltpu.VMEM((slabs_in, STEPS, planes, points), jnp.float32),
            pltpu.VMEM((2, RING - 1, slabs_in, half, width), jnp.float32),
            pltpu.VMEM((2, planes, width), jnp.float32),
            dma((len(inputs),)),
            dma((len(inputs),)),
            dma((2, RING - 1)),
            dma((2, RING - 1)),
            dma((3,)),
            dma((3,)),
            dma((slabs_out, 2, RING - 1)),
            dma((slabs_out, 2, RING - 1)),
            dma((slabs_out, 2, RING)),
            dma((slabs_out, 2, RING)),
        ],
        compiler_params=pltpu.CompilerParams(
            collective_id=collective, has_side_effects=True, vmem_limit_bytes=48 * 1024 * 1024
        ),
        cost_estimate=pl.CostEstimate(flops=0, bytes_accessed=20 * planes * points * 4, transcendentals=0),
    )(*inputs, parcel)


def whole_bands(orbitals, owner, picks):
    bloc, planes, points = orbitals.shape
    half = bloc // 2
    slab = lax.axis_index("slab")
    band = lax.axis_index("band")
    fetched = []
    for step in range(STEPS):
        rows = jnp.stack([lax.dynamic_index_in_dim(orbitals, picks[step, row], 0, keepdims=False) for row in range(2)])
        fetched.append(jnp.where(band == owner[step], rows, jnp.zeros_like(rows)))
    own = lax.dynamic_slice_in_dim(orbitals, slab * half, half, 0)
    sent = lax.dynamic_slice_in_dim(orbitals, (1 - slab) * half, half, 0)
    chosen, other = ring_sum(fetched, sent, 1, 2, 0)
    applied_own, applied_other, summed_own, summed_other = potentials((own, other), chosen)
    summed = [part[step] for part in (summed_own, summed_other) for step in range(STEPS)]
    transposed, back = ring_sum(summed, applied_other, 2, 1, 1)
    exchange = jnp.where(slab == 0, jnp.concatenate([applied_own, back]), jnp.concatenate([back, applied_own]))
    return exchange, transposed[0]


def broadcast(x, axis, root):
    mine = lax.axis_index(axis) == root
    return lax.psum(jnp.where(mine, x, jnp.zeros_like(x)), axis)


def frequency(counter, length):
    return jnp.where(counter <= length // 2, counter, counter - length).astype(jnp.float32)


def coulomb_kernel(freq_z, freq_y, freq_x):
    wave_first = 2.0 * math.pi / length_first
    wave_side = 2.0 * math.pi / length_side
    wave_last = 2.0 * math.pi / length_last
    squared = (
        (wave_first * freq_z)[:, None, None] ** 2
        + (wave_side * freq_y)[None, :, None] ** 2
        + (wave_last * freq_x)[None, None, :] ** 2
    )
    safe = jnp.where(squared > 0, squared, 1.0)
    screened = -4.0 * math.pi * jnp.expm1(-squared / (4.0 * omega_screen**2)) / safe
    return jnp.where(squared > 0, screened, math.pi / omega_screen**2)


def dft_table(length, direction):
    counter = jnp.arange(length)
    product = counter[:, None] * counter[None, :] % length
    angle = 2.0 * math.pi / length * product.astype(jnp.float32)
    return (jnp.cos(angle), direction * jnp.sin(angle))


def along_last(values, length, direction):
    cosines, sine_table = dft_table(length, direction)
    upper = jnp.concatenate([cosines, -sine_table], axis=1)
    lower = jnp.concatenate([sine_table, cosines], axis=1)
    matrix = jnp.concatenate([upper, lower], axis=0)
    return jnp.matmul(values, matrix, precision=lax.Precision.HIGHEST)


def along_axis(values, length, direction, pattern):
    cosines, sine_table = dft_table(length, direction)
    middle = values.shape[-1] // 2
    with_cos = jnp.einsum(pattern, cosines, values, precision=lax.Precision.HIGHEST)
    with_sin = jnp.einsum(pattern, sine_table, values, precision=lax.Precision.HIGHEST)
    real_part = with_cos[..., :middle] + with_sin[..., middle:]
    imag_part = with_cos[..., middle:] - with_sin[..., :middle]
    return jnp.concatenate([real_part, imag_part], axis=-1)


def per_device(orbitals, owner, picks):
    bloc, planes, points = orbitals.shape
    slab_count = lax.axis_size("slab")
    column_rows = NY // slab_count
    slab_index = lax.axis_index("slab")
    freq_y = frequency(slab_index * column_rows + jnp.arange(column_rows), NY)
    kernel = coulomb_kernel(frequency(jnp.arange(NZ), NZ), freq_y, frequency(jnp.arange(NX), NX))
    kernel = kernel * (1.0 / (NX * NY * NZ))
    kernel_tile = jnp.concatenate([kernel, kernel], axis=-1)
    exchange_sum = jnp.zeros_like(orbitals)
    collected = []
    for turn_index in range(STEPS):
        fetch_chosen = jnp.take(orbitals, picks[turn_index], axis=0)
        chosen = broadcast(fetch_chosen, "band", owner[turn_index])
        real_part = (orbitals * chosen[0]).reshape(bloc, planes, NY, NX)
        imag_part = (orbitals * chosen[1]).reshape(bloc, planes, NY, NX)
        fields = jnp.concatenate([real_part, imag_part], axis=-1)
        fields = along_last(fields, NX, 1.0)
        fields = along_axis(fields, NY, 1.0, "ky,bzyx->bzkx")
        columns = lax.all_to_all(fields, "slab", split_axis=2, concat_axis=1, tiled=True)
        columns = along_axis(columns, NZ, 1.0, "kz,bzyx->bkyx") * kernel_tile
        columns = along_axis(columns, NZ, -1.0, "kz,bzyx->bkyx")
        fields = lax.all_to_all(columns, "slab", split_axis=1, concat_axis=2, tiled=True)
        fields = along_axis(fields, NY, -1.0, "ky,bzyx->bzkx")
        fields = along_last(fields, NX, -1.0)
        count = fields.shape[0]
        potentials_first_part = fields[..., :NX].reshape(count, planes, points)
        potentials_second_part = fields[..., NX:].reshape(count, planes, points)
        applied = potentials_first_part * chosen[0] + potentials_second_part * chosen[1]
        contributions_local_sum = jnp.stack(
            [
                jnp.sum(potentials_first_part * orbitals, axis=0),
                jnp.sum(potentials_second_part * orbitals, axis=0),
            ]
        )
        applied, local_sum = (applied, contributions_local_sum)
        exchange_sum = exchange_sum + applied
        collected.append(lax.psum(local_sum, "band"))
    transposed = jnp.stack(collected)
    return (exchange_sum, transposed)


def solution(mesh):
    body = whole_bands if (mesh.shape["band"], mesh.shape["slab"]) == (2 * RING, 2) else per_device
    in_specs = (P("band", "slab", None), P(), P())
    out_specs = (P("band", "slab", None), P(None, None, "slab", None))
    return jax.shard_map(body, mesh=mesh, in_specs=in_specs, out_specs=out_specs, check_vma=False)
```
